256 devices in a mesh: lon: 32 (over x_hi, z, core), tp: 8 (over y, x_lo).
Axes of the slice: x: 4 (x_hi: 2, x_lo: 2; x = x_hi * 2 + x_lo), y: 4, z: 8, core: 2. Of those that a mesh axis runs over, the one named last changes fastest.
Arguments:
- queries: bfloat16 [16384, 3072], P('lon', 'tp'), may hold values from -81 to 81
- keys: bfloat16 [16384, 3072], P('lon', 'tp'), may hold values from -9 to 9
- values: bfloat16 [16384, 3072], P('lon', 'tp'), may hold values from -6 to 6
- out_grad: bfloat16 [16384, 3072], P('lon', 'tp'), may hold values from -6 to 6
- out_weight: bfloat16 [3072, 3072], P('tp'), may hold values from -0.109375 to 0.109375
- window: int32 [128, 9], replicated, may hold values from 0 to 127, as said below
- counts: int32 [128], replicated, may hold values from 1 to 9
Outputs:
- query_grad: bfloat16 [16384, 3072], P('lon', 'tp')
- key_grad: bfloat16 [16384, 3072], P('lon', 'tp')
- value_grad: bfloat16 [16384, 3072], P('lon', 'tp')
- weight_grad: bfloat16 [3072, 3072], P('tp', 'lon')
The draws below stay inside these ranges and needn't reach their ends.
Inputs may be any that keep to these rules, and one draw needn't show every extreme that they name: `window`: for tile g (stripe g // 4, latitude row g % 4) the first counts[g] entries are distinct tiles whose stripe differs from g's by at most one around the loop of 32 stripes and whose latitude row differs by at most one; the first entry is g itself; later entries repeat g.
All inputs are finite; a program needn't handle non-finite values.
Results may differ from the reference program's by a relative error of at most 0.034.
Values may be sent and summed in bfloat16 or wider, within the bound.
A program may use at most 128 MiB of HBM per device.

```python
import jax
import jax.numpy as jnp
from jax import lax

D = 3072
HEADS = 24
HEAD_DIM = 128
TILE = 128
WIN = 9
TPS = 4
TILES = 128
TOKENS = 16384


def shared_rows(key):
    key = jax.random.fold_in(key, 202)
    return jax.random.truncated_normal(key, -4.5, 4.5, (TOKENS, D), jnp.float32)


def window_table(key):
    key = jax.random.fold_in(key, 101)
    stripe_count = TILES // TPS
    tile_all = jnp.arange(TILES, dtype=jnp.int32)
    stripe = tile_all // TPS
    lat_row = tile_all % TPS
    candidate = jnp.arange(9, dtype=jnp.int32)
    move_stripe = candidate // 3 - 1
    move_row = candidate % 3 - 1
    new_row = lat_row[:, None] + move_row[None, :]
    valid = (new_row >= 0) & (new_row < TPS)
    tile_ids = (stripe[:, None] + move_stripe[None, :]) % stripe_count * TPS + jnp.clip(new_row, 0, TPS - 1)
    coin = jax.random.randint(key, (TILES, 9), 0, 4) > 0
    forced = (tile_all % 5 == 2)[:, None]
    centre = (candidate == 4)[None, :]
    chosen = valid & (coin | forced | centre)
    ranking = jnp.where(centre, 0, jnp.where(chosen, 1, 2)).astype(jnp.int32)
    order = jnp.argsort(ranking, axis=1, stable=True)
    picked = jnp.take_along_axis(tile_ids, order, axis=1)
    used = jnp.sum(chosen.astype(jnp.int32), axis=1)
    slots = jnp.arange(WIN, dtype=jnp.int32)
    table = jnp.where(slots[None, :] < used[:, None], picked[:, :WIN], tile_all[:, None])
    return (table.astype(jnp.int32), used.astype(jnp.int32))


def draw_queries(key, part):
    key = jax.random.fold_in(key, 3)
    result = jax.random.truncated_normal(key, -4.5, 4.5, (TOKENS, D), jnp.float32)
    return result.astype(jnp.bfloat16)


def draw_keys(key, part):
    base = shared_rows(key)
    result = base
    return result.astype(jnp.bfloat16)


def draw_window(key, part):
    table, used = window_table(key)
    return table


def draw_counts(key, part):
    table, used = window_table(key)
    return used


def with_spikes(array, own_key, source, target, shards_of, factor):
    def block_of(position):
        return (jnp.arange(array.shape[position]) // (array.shape[position] // shards_of)).reshape((-1,) + (1,) * (array.ndim - 1 - position))

    near = jax.random.permutation(own_key, shards_of)[block_of(target)]
    far = (block_of(target) + shards_of // 2) % shards_of
    return jnp.where((block_of(source) == near) | (block_of(source) == far), factor * array, array)


def block_levels(rng, shape, cuts, smallest, largest):
    gain, own = 1.0, jax.random.fold_in(rng, 6)
    for dim, blocks in cuts:
        heights = jnp.exp(jax.random.uniform(jax.random.fold_in(own, dim), (blocks,), jnp.float32, smallest / len(cuts), largest / len(cuts)))
        gain = gain * jnp.repeat(heights, shape[dim] // blocks).reshape([-1 if axis == dim else 1 for axis in range(len(shape))])
    return gain


def scatter_about(key, extent, width, limit, cuts=(), kind=jnp.bfloat16):
    loudness = block_levels(key, extent, cuts, -0.22, 0.18) if cuts else 1.0
    array = jax.random.normal(key, extent, jnp.float32) * width * loudness
    return jnp.minimum(jnp.maximum(array, -limit), limit).astype(kind)


def bell_draw_with(stream_key, shape, deviation, limit, pieces, heavy, held_as=jnp.bfloat16):
    entries = deviation * jax.random.normal(stream_key, shape, jnp.float32)
    if pieces:
        entries = entries * block_levels(stream_key, shape, pieces, -0.22, 0.18)
    return jnp.clip(with_spikes(entries, jax.random.fold_in(stream_key, 3), *heavy), -limit, limit).astype(held_as)


def setup_inputs(seed: int = 0) -> dict:
    splits = jax.random.split(jax.random.key(seed), 8)
    queries = draw_queries(jax.random.fold_in(splits[7], 71), 0)
    keys = draw_keys(jax.random.fold_in(splits[7], 71), 0)
    values = scatter_about(splits[2], (TOKENS, D), 1.0, 6.0, ((0, 32), (1, 8)))
    out_grad = bell_draw_with(splits[3], (TOKENS, D), 1.0, 6.0, ((0, 32), (1, 8)), (0, 1, 32, 2.75))
    out_weight = scatter_about(splits[4], (D, D), D ** -0.5, 0.109375, ((0, 8),))
    window = draw_window(jax.random.fold_in(splits[7], 71), 0)
    counts = draw_counts(jax.random.fold_in(splits[7], 71), 0)
    return {"queries": queries, "keys": keys, "values": values, "out_grad": out_grad, "out_weight": out_weight, "window": window, "counts": counts}


neg_fill = -1.0e30


def reference(queries, keys, values, out_grad, out_weight, window, counts):
    tiles_all = TOKENS // TILE
    inv_root = HEAD_DIM ** -0.5
    query_tiles = queries.reshape(tiles_all, TILE, HEADS, HEAD_DIM)
    key_tiles = keys.reshape(tiles_all, TILE, HEADS, HEAD_DIM)
    value_tiles = values.reshape(tiles_all, TILE, HEADS, HEAD_DIM)
    slots = jnp.arange(WIN, dtype=jnp.int32)

    def tile_probs(tile_no):
        tile_ids = window[tile_no].astype(jnp.int32)
        slot_live = slots < counts[tile_no]
        near_keys = key_tiles[tile_ids].reshape(WIN * TILE, HEADS, HEAD_DIM).astype(jnp.float32)
        near_values = value_tiles[tile_ids].reshape(WIN * TILE, HEADS, HEAD_DIM).astype(jnp.float32)
        keep = jnp.repeat(slot_live, TILE)
        scores = jnp.einsum("qhd,khd->hqk", query_tiles[tile_no].astype(jnp.float32), near_keys) * inv_root
        scores = jnp.where(keep[None, None, :], scores, neg_fill)
        row_max = jnp.max(scores, axis=2, keepdims=True)
        weights = jnp.exp(scores - row_max)
        probs = weights / jnp.sum(weights, axis=2, keepdims=True)
        return tile_ids, slot_live, near_keys, near_values, probs

    def forward_tile(tile_no):
        tile_ids, slot_live, near_keys, near_values, probs = tile_probs(tile_no)
        probs_low = lax.optimization_barrier(probs.astype(jnp.bfloat16)).astype(jnp.float32)
        return jnp.einsum("hqk,khd->qhd", probs_low, near_values).astype(jnp.bfloat16)

    attended = lax.map(forward_tile, jnp.arange(tiles_all, dtype=jnp.int32)).reshape(TOKENS, D)
    grad_attended = jnp.dot(out_grad, out_weight.T, preferred_element_type=jnp.float32).astype(jnp.bfloat16)
    weight_grad = jnp.dot(attended.T, out_grad, preferred_element_type=jnp.float32).astype(jnp.bfloat16)
    grad_tiles = grad_attended.reshape(tiles_all, TILE, HEADS, HEAD_DIM)
    attended_tiles = attended.reshape(tiles_all, TILE, HEADS, HEAD_DIM)

    def backward_tile(carry, tile_no):
        key_total, value_total = carry
        tile_ids, slot_live, near_keys, near_values, probs = tile_probs(tile_no)
        grad_here = grad_tiles[tile_no].astype(jnp.float32)
        delta = jnp.sum(grad_here * attended_tiles[tile_no].astype(jnp.float32), axis=2)
        grad_probs = jnp.einsum("qhd,khd->hqk", grad_here, near_values)
        grad_scores = probs * (grad_probs - delta.T[:, :, None])
        grad_scores = lax.optimization_barrier(grad_scores.astype(jnp.bfloat16)).astype(jnp.float32)
        probs_low = lax.optimization_barrier(probs.astype(jnp.bfloat16)).astype(jnp.float32)
        query_part = (jnp.einsum("hqk,khd->qhd", grad_scores, near_keys) * inv_root).astype(jnp.bfloat16)
        key_part = jnp.einsum("hqk,qhd->khd", grad_scores, query_tiles[tile_no].astype(jnp.float32)) * inv_root
        value_part = jnp.einsum("hqk,qhd->khd", probs_low, grad_here)
        slot_weight = jnp.repeat(slot_live, TILE).astype(jnp.float32)[:, None, None]
        key_part = (key_part * slot_weight).reshape(WIN, TILE, D)
        value_part = (value_part * slot_weight).reshape(WIN, TILE, D)
        key_total = key_total.at[tile_ids].add(key_part)
        value_total = value_total.at[tile_ids].add(value_part)
        return (key_total, value_total), query_part

    empty = jnp.zeros((tiles_all, TILE, D), jnp.float32)
    (key_total, value_total), query_parts = lax.scan(backward_tile, (empty, empty), jnp.arange(tiles_all, dtype=jnp.int32))
    query_grad = query_parts.reshape(TOKENS, D)
    key_grad = key_total.reshape(TOKENS, D).astype(jnp.bfloat16)
    value_grad = value_total.reshape(TOKENS, D).astype(jnp.bfloat16)
    return query_grad, key_grad, value_grad, weight_grad
```

```python
import jax
import jax.numpy as jnp
from jax import lax
from jax.experimental import pallas as pl
from jax.experimental.pallas import tpu as pltpu
from jax.sharding import PartitionSpec as P

MESH = pl.DeviceIdType.MESH
F32 = jnp.float32
BF16 = jnp.bfloat16
HEAD_DIM = 128
TILE = 128
HEADS_HERE = 3
TOK = 512
COLS = HEADS_HERE * HEAD_DIM
SPAN = 3 * TILE
HALF = 2 * TILE
WIN = 9
LON = 32
TP = 8
STRIP = 96
INV_ROOT = HEAD_DIM ** -0.5
LOG2E = 1.4426950408889634
NEG = -1e30

NT = (((1,), (1,)), ((), ()))


def dot(a, b):
    return jnp.dot(a, b, preferred_element_type=F32)


def kernel(
    win_ref, cnt_ref, q_hbm, k_hbm, v_hbm, og_hbm, w_hbm,
    dq_ref, dk_ref, dv_ref, wg_ref,
    q_v, k_all, v_all, og_v, w_v, og_t, k_t, v_t, prob, scores, bias,
    att_t, att, inv_sum, delta, do_acc, do_t, do_n, dq_acc, pair_acc,
    own_pair, pair_out, pair_in, wg_full, wg_own, core_out, core_in,
    up_out, up_in, down_out, down_in, x_out, x_in,
    loc_sem, halo_s, halo_r, ag_s, ag_r, pair_s, pair_r, core_s, core_r,
    up_s, up_r, down_s, down_r, x_s, x_r,
):
    lon = lax.axis_index("lon")
    tp = lax.axis_index("tp")
    x_hi = lax.div(lon, 16)
    z = lax.rem(lax.div(lon, 2), 8)
    core = lax.rem(lon, 2)
    y = lax.div(tp, 2)
    x_lo = lax.rem(tp, 2)

    right = {"lon": lax.rem(lon + 1, LON)}
    left = {"lon": lax.rem(lon + LON - 1, LON)}
    twin = {"lon": lon + 1 - 2 * core}
    z_up = {"lon": x_hi * 16 + lax.rem(z + 1, 8) * 2 + core}
    z_down = {"lon": x_hi * 16 + lax.rem(z + 7, 8) * 2 + core}
    x_far = {"lon": lax.rem(lon + 16, LON)}
    y_p = lax.rem(y + 1, 4)
    y_m = lax.rem(y + 3, 4)
    y_2 = lax.rem(y + 2, 4)
    s_x = y * 2 + 1 - x_lo
    s_p = y_p * 2 + x_lo
    s_m = y_m * 2 + x_lo
    s_2 = y_2 * 2 + x_lo
    s_px = y_p * 2 + 1 - x_lo
    s_mx = y_m * 2 + 1 - x_lo
    s_2x = y_2 * 2 + 1 - x_lo
    to_x, to_p, to_m = {"tp": s_x}, {"tp": s_p}, {"tp": s_m}

    barrier = pltpu.get_barrier_semaphore()
    for other in (right, left, z_up, z_down, x_far, to_x, to_p, to_m):
        pl.semaphore_signal(barrier, inc=1, device_id=other, device_id_type=MESH)

    local = [
        pltpu.make_async_copy(src, dst, loc_sem.at[i])
        for i, (src, dst) in enumerate(
            ((og_hbm, og_v), (q_hbm, q_v), (k_hbm, k_all.at[1]), (v_hbm, v_all.at[1]), (w_hbm, w_v))
        )
    ]
    for copy in local:
        copy.start()
    local[0].wait()
    og_t[tp] = og_v[...].T

    def remote(src, dst, send, recv, to):
        return pltpu.make_async_remote_copy(
            src_ref=src, dst_ref=dst, send_sem=send, recv_sem=recv, device_id=to, device_id_type=MESH
        )

    def gather(number, slot, half, to):
        block = og_t.at[slot, pl.ds(half * 192, 192)]
        return remote(block, block, ag_s.at[number], ag_r.at[number], to)

    pl.semaphore_wait(barrier, 8)
    x0 = [gather(h, tp, h, to_x) for h in range(2)]
    p0 = [gather(2 + h, tp, h, to_p) for h in range(2)]
    m0 = [gather(4 + h, tp, h, to_m) for h in range(2)]
    x1 = [gather(6 + h, s_p, h, to_x) for h in range(2)]
    m1 = gather(8, s_p, 0, to_m)
    p1 = gather(9, s_m, 1, to_p)
    p2 = [gather(10 + h, s_x, h, to_p) for h in range(2)]
    m2 = [gather(12 + h, s_px, h, to_m) for h in range(2)]
    halo = [
        remote(k_hbm, k_all.at[0], halo_s.at[0], halo_r.at[0], right),
        remote(k_hbm, k_all.at[2], halo_s.at[1], halo_r.at[1], left),
        remote(v_hbm, v_all.at[0], halo_s.at[2], halo_r.at[2], right),
        remote(v_hbm, v_all.at[2], halo_s.at[3], halo_r.at[3], left),
    ]
    for h in range(2):
        x0[h].start()
        p0[h].start()
        m0[h].start()
    for copy in halo:
        copy.start()

    lane = lax.broadcasted_iota(jnp.int32, (1, HALF), 1)
    words = []
    for t in range(4):
        tile = lon * 4 + t
        word = jnp.int32(0)
        for slot in range(WIN):
            other = win_ref[slot, tile]
            place = lax.rem(lax.div(other, 4) + (LON + 1) - lon, LON) * 4 + lax.rem(other, 4)
            live = (slot < cnt_ref[tile]).astype(jnp.int32)
            word = word | lax.shift_left(live, place)
        words.append(word)
    for a in range(2):
        for n in range(3):
            for r in range(3):
                code = n * 4 + a + r
                fill = [
                    jnp.where((lax.shift_right_logical(words[2 * a + i], jnp.int32(code)) & 1) == 1, 0.0, NEG)
                    for i in range(2)
                ]
                bias[a, n * 3 + r : n * 3 + r + 1, :] = jnp.where(lane < TILE, fill[0], fill[1]).astype(F32)

    for copy in local[1:]:
        copy.wait()
    k_t[1] = k_all[1].T
    v_t[1] = v_all[1].T

    m0[0].wait_recv()
    x1[0].start()
    m1.start()
    x0[0].wait_recv()
    p2[0].start()
    m0[1].wait_recv()
    x1[1].start()
    p0[0].wait_recv()
    p0[1].wait_recv()
    p1.start()
    x0[1].wait_recv()
    p2[1].start()

    for copy in halo:
        copy.wait_recv()
    for n in (0, 2):
        k_t[n] = k_all[n].T
        v_t[n] = v_all[n].T

    def forward(h, carry):
        cols = pl.ds(pl.multiple_of(h * HEAD_DIM, HEAD_DIM), HEAD_DIM)
        for a in range(2):
            here = slice(a * HALF, (a + 1) * HALF)
            keys = slice(a * TILE, a * TILE + SPAN)
            q = q_v[here, cols]
            top = None
            for n in range(3):
                s = lax.dot_general(k_all[n, keys, cols], q, NT, preferred_element_type=F32)
                s = s.reshape(3, TILE, HALF) * (INV_ROOT * LOG2E) + bias[a, n * 3 : n * 3 + 3][:, None, :]
                s = s.reshape(SPAN, HALF)
                scores[n] = s
                peak = jnp.max(s, axis=0, keepdims=True)
                top = peak if top is None else jnp.maximum(top, peak)
            total = jnp.zeros((1, HALF), F32)
            out = jnp.zeros((HEAD_DIM, HALF), F32)
            for n in range(3):
                e = jnp.exp2(scores[n] - top)
                total += jnp.sum(e, axis=0, keepdims=True)
                low = e.astype(BF16)
                prob[h, n, a] = low
                out += dot(v_t[n, cols, keys], low)
            inverse = 1.0 / total
            inv_sum[h, :, here] = inverse
            att_t[cols, here] = (out * inverse).astype(BF16)

        @pl.when(h < 2)
        def _():
            for i in range(2):
                @pl.when(h == i)
                def _():
                    x1[i].wait_recv()
                    m2[i].start()

        return carry

    lax.fori_loop(0, HEADS_HERE, forward, 0)
    att[...] = att_t[...].T

    core_copies = []

    def use_piece(order, piece):
        block = og_t[piece]
        part = dot(w_v[:, pl.ds(pl.multiple_of(piece * COLS, COLS), COLS)], block)
        if order == 0:
            do_acc[...] = part
        else:
            do_acc[...] += part
        wg_full[...] = dot(block, att[...])
        for j in range(2):
            wg_own[piece * 2 + j] = wg_full[pl.ds(pl.multiple_of((2 * j + core) * STRIP, STRIP), STRIP)]
            core_out[piece * 2 + j] = wg_full[
                pl.ds(pl.multiple_of((2 * j + 1 - core) * STRIP, STRIP), STRIP)
            ].astype(BF16)
        both = pl.ds(piece * 2, 2)
        copy = remote(core_out.at[both], core_in.at[both], core_s.at[order], core_r.at[order], twin)
        copy.start()
        core_copies.append(copy)

    for order, piece in enumerate((tp, s_x, s_p, s_m, s_px)):
        use_piece(order, piece)
    m1.wait_recv()
    p1.wait_recv()
    use_piece(5, s_2)
    for copy in p2:
        copy.wait_recv()
    use_piece(6, s_mx)
    for copy in m2:
        copy.wait_recv()
    use_piece(7, s_2x)

    for h in range(HEADS_HERE):
        rows = slice(h * HEAD_DIM, (h + 1) * HEAD_DIM)
        scaled = (do_acc[rows] * inv_sum[h]).astype(BF16)
        do_t[rows] = scaled
        delta[h] = jnp.sum(scaled.astype(F32) * att_t[rows].astype(F32), axis=0, keepdims=True)
    do_n[...] = do_t[...].T

    for copy in core_copies:
        copy.wait_recv()

    def share(block):
        return wg_own[block] + core_in[block].astype(F32)

    up_copies, down_copies = [], []

    def ring(s):
        if s > 0:
            up_copies[s - 1].wait_recv()
            down_copies[s - 1].wait_recv()
        up_z = lax.rem(z + 4 - s, 8)
        down_z = lax.rem(z + 4 + s, 8)
        for x in range(2):
            if s > 0 or x == 0:
                value = share(x * 8 + up_z)
                if s > 1 or (s == 1 and x == 0):
                    value += up_in[s - 1, x].astype(F32)
                up_out[s, x] = value.astype(BF16)
            if s > 0 or x == 1:
                value = share(x * 8 + down_z)
                if s > 1 or (s == 1 and x == 1):
                    value += down_in[s - 1, x].astype(F32)
                down_out[s, x] = value.astype(BF16)
        if s == 0:
            up = remote(up_out.at[0, 0], up_in.at[0, 0], up_s.at[0], up_r.at[0], z_up)
            down = remote(down_out.at[0, 1], down_in.at[0, 1], down_s.at[0], down_r.at[0], z_down)
        else:
            up = remote(up_out.at[s], up_in.at[s], up_s.at[s], up_r.at[s], z_up)
            down = remote(down_out.at[s], down_in.at[s], down_s.at[s], down_r.at[s], z_down)
        up.start()
        down.start()
        up_copies.append(up)
        down_copies.append(down)

    ring(0)
    pair_copies = []

    def backward(h):
        cols = slice(h * HEAD_DIM, (h + 1) * HEAD_DIM)
        for n in (0, 2, 1):
            for a in range(2):
                here = slice(a * HALF, (a + 1) * HALF)
                keys = slice(a * TILE, a * TILE + SPAN)
                low = prob[h, n, a]
                dp = dot(v_all[n, keys, cols], do_t[cols, here])
                ds = (low.astype(F32) * (dp - delta[h, :, here])).astype(BF16)
                dkey = dot(ds, q_v[here, cols])
                dval = dot(low, do_n[here, cols])
                dquery = dot(k_t[n, cols, keys], ds)
                if n == 0:
                    dq_acc[:, here] = dquery
                else:
                    dq_acc[:, here] += dquery
                if a == 0:
                    pair_acc[0:SPAN, 0:HEAD_DIM] = dkey
                    pair_acc[0:SPAN, HEAD_DIM:] = dval
                else:
                    pair_acc[TILE:SPAN, 0:HEAD_DIM] += dkey[:HALF]
                    pair_acc[TILE:SPAN, HEAD_DIM:] += dval[:HALF]
                    pair_acc[SPAN:, 0:HEAD_DIM] = dkey[HALF:]
                    pair_acc[SPAN:, HEAD_DIM:] = dval[HALF:]
            if n == 1:
                own_pair[h] = pair_acc[...]
            else:
                way = n // 2
                pair_out[way, h] = pair_acc[...].astype(BF16)
                number = h * 2 + way
                copy = remote(
                    pair_out.at[way, h], pair_in.at[way, h], pair_s.at[number], pair_r.at[number],
                    right if way else left,
                )
                copy.start()
                pair_copies.append(copy)
        dq_ref[:, cols] = (dq_acc[...] * INV_ROOT).astype(BF16).T

    for h in range(HEADS_HERE):
        backward(h)
        ring(h + 1)

    up_copies[3].wait_recv()
    down_copies[3].wait_recv()

    def gathered(x):
        return share(x * 8 + z) + up_in[3, x].astype(F32) + down_in[3, x].astype(F32)

    x_out[...] = gathered(1 - x_hi).astype(BF16)
    swap = remote(x_out, x_in, x_s.at[0], x_r.at[0], x_far)
    swap.start()

    for h in range(HEADS_HERE):
        cols = slice(h * HEAD_DIM, (h + 1) * HEAD_DIM)
        pair_copies[2 * h].wait_recv()
        pair_copies[2 * h + 1].wait_recv()
        total = own_pair[h] + pair_in[0, h].astype(F32) + pair_in[1, h].astype(F32)
        dk_ref[:, cols] = (total[:, :HEAD_DIM] * INV_ROOT).astype(BF16)
        dv_ref[:, cols] = total[:, HEAD_DIM:].astype(BF16)

    swap.wait_recv()
    wg_ref[...] = (gathered(x_hi) + x_in[...].astype(F32)).astype(BF16)

    for copy in (*x0, *p0, *m0, *x1, m1, p1, *p2, *m2, *halo, *core_copies, *up_copies, *down_copies, *pair_copies, swap):
        copy.wait_send()


def body(queries, keys, values, out_grad, out_weight, window, counts):
    hbm = pl.BlockSpec(memory_space=pl.ANY)
    vmem = pl.BlockSpec(memory_space=pltpu.VMEM)
    smem = pl.BlockSpec(memory_space=pltpu.SMEM)
    V = pltpu.VMEM
    dma = pltpu.SemaphoreType.DMA
    block = jax.ShapeDtypeStruct((TOK, COLS), BF16)
    scratch = [
        V((TOK, COLS), BF16),
        V((3, TOK, COLS), BF16),
        V((3, TOK, COLS), BF16),
        V((TOK, COLS), BF16),
        V((COLS, TP * COLS), BF16),
        V((TP, COLS, TOK), BF16),
        V((3, COLS, TOK), BF16),
        V((3, COLS, TOK), BF16),
        V((HEADS_HERE, 3, 2, SPAN, HALF), BF16),
        V((3, SPAN, HALF), F32),
        V((2, 16, HALF), F32),
        V((COLS, TOK), BF16),
        V((TOK, COLS), BF16),
        V((HEADS_HERE, 1, TOK), F32),
        V((HEADS_HERE, 1, TOK), F32),
        V((COLS, TOK), F32),
        V((COLS, TOK), BF16),
        V((TOK, COLS), BF16),
        V((HEAD_DIM, TOK), F32),
        V((TOK, HALF), F32),
        V((HEADS_HERE, TOK, HALF), F32),
        V((2, HEADS_HERE, TOK, HALF), BF16),
        V((2, HEADS_HERE, TOK, HALF), BF16),
        V((COLS, COLS), F32),
        V((16, STRIP, COLS), F32),
        V((16, STRIP, COLS), BF16),
        V((16, STRIP, COLS), BF16),
        V((4, 2, STRIP, COLS), BF16),
        V((4, 2, STRIP, COLS), BF16),
        V((4, 2, STRIP, COLS), BF16),
        V((4, 2, STRIP, COLS), BF16),
        V((STRIP, COLS), BF16),
        V((STRIP, COLS), BF16),
        dma((5,)),
        dma((4,)), dma((4,)),
        dma((14,)), dma((14,)),
        dma((6,)), dma((6,)),
        dma((8,)), dma((8,)),
        dma((4,)), dma((4,)),
        dma((4,)), dma((4,)),
        dma((1,)), dma((1,)),
    ]
    dq, dk, dv, wg = pl.pallas_call(
        kernel,
        out_shape=(block, block, block, jax.ShapeDtypeStruct((STRIP, COLS), BF16)),
        in_specs=[smem, smem, hbm, hbm, hbm, hbm, hbm],
        out_specs=(vmem, vmem, vmem, vmem),
        scratch_shapes=scratch,
        compiler_params=pltpu.CompilerParams(
            collective_id=0, has_side_effects=True, vmem_limit_bytes=56 * 1024 * 1024
        ),
    )(window.T, counts, queries, keys, values, out_grad, out_weight)
    return dq, dk, dv, wg.T


def solution(mesh):
    in_specs = (
        P("lon", "tp"),
        P("lon", "tp"),
        P("lon", "tp"),
        P("lon", "tp"),
        P("tp", None),
        P(),
        P(),
    )
    out_specs = (P("lon", "tp"), P("lon", "tp"), P("lon", "tp"), P("tp", "lon"))
    return jax.shard_map(body, mesh=mesh, in_specs=in_specs, out_specs=out_specs, check_vma=False)
```

```python
import jax
import jax.numpy as jnp
from jax import lax
from jax.experimental import pallas as pl
from jax.experimental.pallas import tpu as pltpu
from jax.sharding import PartitionSpec as P

MESH = pl.DeviceIdType.MESH
F32 = jnp.float32
BF16 = jnp.bfloat16
HEAD_DIM = 128
TILE = 128
HEADS_HERE = 3
TOK = 512
COLS = HEADS_HERE * HEAD_DIM
SPAN = 3 * TILE
HALF = 2 * TILE
WIN = 9
LON = 32
TP = 8
STRIP = 96
GATHERS = 28
INV_ROOT = HEAD_DIM ** -0.5
LOG2E = 1.4426950408889634
NEG = -1e30

NT = (((1,), (1,)), ((), ()))


def dot(a, b):
    return jnp.dot(a, b, preferred_element_type=F32)


def kernel(
    win_ref, cnt_ref, q_hbm, k_hbm, v_hbm, og_hbm, w_hbm,
    dq_ref, dk_ref, dv_ref, wg_ref,
    q_v, k_all, v_all, og_v, w_v, og_t, k_t, v_t, prob, scores, bias,
    att_t, att, inv_sum, delta, do_acc, do_t, do_n, dq_acc, pair_acc,
    own_pair, pair_out, pair_in, wg_full, wg_own, core_out, core_in,
    ring_out, ring_in, x_out, x_in,
    loc_sem, halo_s, halo_r, ag_s, ag_r, pair_s, pair_r, core_s, core_r,
    ring_s, ring_r, x_s, x_r,
):
    lon = lax.axis_index("lon")
    tp = lax.axis_index("tp")
    x_hi = lax.div(lon, 16)
    z = lax.rem(lax.div(lon, 2), 8)
    core = lax.rem(lon, 2)
    y = lax.div(tp, 2)
    x_lo = lax.rem(tp, 2)

    right = {"lon": lax.rem(lon + 1, LON)}
    left = {"lon": lax.rem(lon + LON - 1, LON)}
    twin = {"lon": lon + 1 - 2 * core}
    z_up = {"lon": x_hi * 16 + lax.rem(z + 1, 8) * 2 + core}
    z_down = {"lon": x_hi * 16 + lax.rem(z + 7, 8) * 2 + core}
    x_far = {"lon": lax.rem(lon + 16, LON)}
    up_far = {"lon": (1 - x_hi) * 16 + lax.rem(z + 1, 8) * 2 + core}
    down_far = {"lon": (1 - x_hi) * 16 + lax.rem(z + 7, 8) * 2 + core}
    y_p = lax.rem(y + 1, 4)
    y_m = lax.rem(y + 3, 4)
    y_2 = lax.rem(y + 2, 4)
    s_x = y * 2 + 1 - x_lo
    s_p = y_p * 2 + x_lo
    s_m = y_m * 2 + x_lo
    s_2 = y_2 * 2 + x_lo
    s_px = y_p * 2 + 1 - x_lo
    s_mx = y_m * 2 + 1 - x_lo
    s_2x = y_2 * 2 + 1 - x_lo
    to_x, to_p, to_m = {"tp": s_x}, {"tp": s_p}, {"tp": s_m}

    barrier = pltpu.get_barrier_semaphore()
    for other in (right, left, z_up, z_down, x_far, up_far, down_far, to_x, to_p, to_m):
        pl.semaphore_signal(barrier, inc=1, device_id=other, device_id_type=MESH)

    def head(h):
        return slice(h * HEAD_DIM, (h + 1) * HEAD_DIM)

    local_og = pltpu.make_async_copy(og_hbm, og_v, loc_sem.at[0])
    local_kv = [
        pltpu.make_async_copy(src.at[:, head(h)], dst.at[1, h], loc_sem.at[1 + 2 * h + i])
        for h in range(HEADS_HERE)
        for i, (src, dst) in enumerate(((k_hbm, k_all), (v_hbm, v_all)))
    ]
    local_q = pltpu.make_async_copy(q_hbm, q_v, loc_sem.at[7])
    local_w = pltpu.make_async_copy(w_hbm, w_v, loc_sem.at[8])
    for copy in (local_og, *local_kv, local_q, local_w):
        copy.start()

    sent = []

    def remote(src, dst, send, recv, to):
        copy = pltpu.make_async_remote_copy(
            src_ref=src, dst_ref=dst, send_sem=send, recv_sem=recv, device_id=to, device_id_type=MESH
        )
        sent.append(copy)
        return copy

    count = iter(range(GATHERS))

    def gather(slot, quarter, to):
        block = og_t.at[slot, pl.ds(quarter * STRIP, STRIP)]
        number = next(count)
        return remote(block, block, ag_s.at[number], ag_r.at[number], to)

    x0 = {i: gather(tp, i, to_x) for i in (0, 1, 2, 3)}
    p0 = {i: gather(tp, i, to_p) for i in (2, 3, 0, 1)}
    m0 = {i: gather(tp, i, to_m) for i in (0, 1, 2, 3)}
    p1 = {i: gather(s_m, i, to_p) for i in (2, 3)}
    m1 = {i: gather(s_p, i, to_m) for i in (0, 1)}
    p2 = {i: gather(s_x, i, to_p) for i in (2, 3, 1)}
    m2 = {i: gather(s_x, i, to_m) for i in (0, 1, 2)}
    x1 = {3: gather(s_p, 3, to_x)}
    x2 = {0: gather(s_m, 0, to_x)}
    p3 = {i: gather(s_mx, i, to_p) for i in (2, 3)}
    m3 = {i: gather(s_px, i, to_m) for i in (0, 1)}

    halo = []
    for h in range(HEADS_HERE):
        part = []
        for i, ref in enumerate((k_all, v_all)):
            for j, to in enumerate((right, left)):
                number = h * 4 + i * 2 + j
                part.append(
                    remote(ref.at[1, h], ref.at[2 * j, h], halo_s.at[number], halo_r.at[number], to)
                )
        halo.append(part)

    local_og.wait()
    og_t[tp] = og_v[...].T
    for copy in (*local_kv, local_q):
        copy.wait()
    pl.semaphore_wait(barrier, 10)
    for i, (a, b, c) in enumerate(zip(x0.values(), p0.values(), m0.values(), strict=True)):
        a.start()
        b.start()
        c.start()

    around = (lax.rem(lon, 16) == 15, lax.rem(lon, 16) == 0)

    def send_halo(late):
        for j in range(2):
            @pl.when(around[j] if late else jnp.logical_not(around[j]))
            def _():
                for h in range(HEADS_HERE):
                    halo[h][j].start()
                    halo[h][2 + j].start()

    send_halo(False)

    lane = lax.broadcasted_iota(jnp.int32, (1, HALF), 1)
    words = []
    for t in range(4):
        tile = lon * 4 + t
        word = jnp.int32(0)
        for slot in range(WIN):
            other = win_ref[slot, tile]
            place = lax.rem(lax.div(other, 4) + (LON + 1) - lon, LON) * 4 + lax.rem(other, 4)
            live = (slot < cnt_ref[tile]).astype(jnp.int32)
            word = word | lax.shift_left(live, place)
        words.append(word)
    for a in range(2):
        for n in range(3):
            for r in range(3):
                code = n * 4 + a + r
                fill = [
                    jnp.where((lax.shift_right_logical(words[2 * a + i], jnp.int32(code)) & 1) == 1, 0.0, NEG)
                    for i in range(2)
                ]
                bias[a, n * 3 + r : n * 3 + r + 1, :] = jnp.where(lane < TILE, fill[0], fill[1]).astype(F32)

    for h in range(HEADS_HERE):
        k_t[1, h] = k_all[1, h].T
        v_t[1, h] = v_all[1, h].T

    def forward(h, a):
        cols = head(h)
        here = slice(a * HALF, (a + 1) * HALF)
        keys = slice(a * TILE, a * TILE + SPAN)
        q = q_v[here, cols]
        top = None
        for n in range(3):
            s = lax.dot_general(k_all[n, h, keys, :], q, NT, preferred_element_type=F32)
            s = s.reshape(3, TILE, HALF) * (INV_ROOT * LOG2E) + bias[a, n * 3 : n * 3 + 3][:, None, :]
            s = s.reshape(SPAN, HALF)
            scores[n] = s
            peak = jnp.max(s, axis=0, keepdims=True)
            top = peak if top is None else jnp.maximum(top, peak)
        total = jnp.zeros((1, HALF), F32)
        out = jnp.zeros((HEAD_DIM, HALF), F32)
        for n in range(3):
            e = jnp.exp2(scores[n] - top)
            total += jnp.sum(e, axis=0, keepdims=True)
            low = e.astype(BF16)
            prob[h, n, a] = low
            out += dot(v_t[n, h, :, keys], low)
        inverse = 1.0 / total
        inv_sum[h, :, here] = inverse
        att_t[cols, here] = (out * inverse).astype(BF16)

    def passed(before, after):
        for copy in before:
            copy.wait_recv()
        for copy in after:
            copy.start()

    passed((p0[2], p0[3], m0[0], m0[1]), (*p1.values(), *m1.values()))
    passed((x0[0], x0[1], x0[2]), (p2[2], m2[0], m2[1], p2[1]))
    passed((x0[3],), (p2[3], m2[2]))
    send_halo(True)
    passed((m0[2], m0[3], p0[0], p0[1]), (x1[3], x2[0]))

    for h in range(HEADS_HERE):
        for copy in halo[h]:
            copy.wait_recv()
        for n in (0, 2):
            v_t[n, h] = v_all[n, h].T
        forward(h, 0)
        forward(h, 1)
    passed((p2[2], m2[0]), (p3[2], m3[0]))
    passed((p2[3], m2[1]), (p3[3], m3[1]))
    att[...] = att_t[...].T
    for h in range(HEADS_HERE):
        for n in (0, 2):
            k_t[n, h] = k_all[n, h].T

    core_copies = []

    def use_piece(order, piece):
        block = og_t[piece]
        part = dot(w_v[:, pl.ds(pl.multiple_of(piece * COLS, COLS), COLS)], block)
        if order == 0:
            do_acc[...] = part
        else:
            do_acc[...] += part
        wg_full[...] = dot(block, att[...])
        for j in range(2):
            wg_own[piece * 2 + j] = wg_full[pl.ds(pl.multiple_of((2 * j + core) * STRIP, STRIP), STRIP)]
            core_out[piece * 2 + j] = wg_full[
                pl.ds(pl.multiple_of((2 * j + 1 - core) * STRIP, STRIP), STRIP)
            ].astype(BF16)
        both = pl.ds(piece * 2, 2)
        copy = remote(core_out.at[both], core_in.at[both], core_s.at[order], core_r.at[order], twin)
        copy.start()
        core_copies.append(copy)

    local_w.wait()
    use_piece(0, tp)
    use_piece(1, s_x)
    use_piece(2, s_p)
    use_piece(3, s_m)
    passed((*p1.values(), *m1.values()), ())
    use_piece(4, s_2)
    passed((x1[3], m2[2]), ())
    use_piece(5, s_px)
    passed((x2[0], p2[1]), ())
    use_piece(6, s_mx)
    passed((*p3.values(), *m3.values()), ())
    use_piece(7, s_2x)

    for h in range(HEADS_HERE):
        rows = head(h)
        scaled = (do_acc[rows] * inv_sum[h]).astype(BF16)
        do_t[rows] = scaled
        delta[h] = jnp.sum(scaled.astype(F32) * att_t[rows].astype(F32), axis=0, keepdims=True)
    do_n[...] = do_t[...].T

    for copy in core_copies:
        copy.wait_recv()

    def share(block):
        return wg_own[block] + core_in[block].astype(F32)

    chains = {}

    def chain(way, x, s):
        first = s == (0 if way == x else 1)
        step = lax.rem(z + (4 - s if way == 0 else 4 + s), 8)
        value = share(x * 8 + step)
        if not first:
            chains[way, x, s - 1].wait_recv()
            value += ring_in[way, x, s - 1].astype(F32)
        ring_out[way, x, s] = value.astype(BF16)
        number = way * 8 + x * 4 + s
        if s < 3:
            copy = remote(
                ring_out.at[way, x, s], ring_in.at[way, x, s], ring_s.at[number], ring_r.at[number],
                z_down if way else z_up,
            )
        else:
            copy = remote(
                ring_out.at[way, x, s], ring_in.at[way, x_hi, s], ring_s.at[number], ring_r.at[way * 8 + x_hi * 4 + s],
                {"lon": x * 16 + lax.rem(z + (7 if way else 1), 8) * 2 + core},
            )
        copy.start()
        chains[way, x, s] = copy

    def ring(point):
        chain(0, 0, point)
        chain(1, 1, point)
        if point < 3:
            chain(0, 1, point + 1)
            chain(1, 0, point + 1)

    pair_copies = {}

    def backward(h, n):
        cols = head(h)
        for a in range(2):
            here = slice(a * HALF, (a + 1) * HALF)
            keys = slice(a * TILE, a * TILE + SPAN)
            low = prob[h, n, a]
            dp = dot(v_all[n, h, keys, :], do_t[cols, here])
            ds = (low.astype(F32) * (dp - delta[h, :, here])).astype(BF16)
            dkey = dot(ds, q_v[here, cols])
            dval = dot(low, do_n[here, cols])
            dquery = dot(k_t[n, h, :, keys], ds)
            if n == 0:
                dq_acc[h, :, here] = dquery
            else:
                dq_acc[h, :, here] += dquery
            if a == 0:
                pair_acc[0:SPAN, 0:HEAD_DIM] = dkey
                pair_acc[0:SPAN, HEAD_DIM:] = dval
            else:
                pair_acc[TILE:SPAN, 0:HEAD_DIM] += dkey[:HALF]
                pair_acc[TILE:SPAN, HEAD_DIM:] += dval[:HALF]
                pair_acc[SPAN:, 0:HEAD_DIM] = dkey[HALF:]
                pair_acc[SPAN:, HEAD_DIM:] = dval[HALF:]
        if n == 1:
            own_pair[h] = pair_acc[...]
        else:
            way = n // 2
            pair_out[way, h] = pair_acc[...].astype(BF16)
            number = h * 2 + way
            copy = remote(
                pair_out.at[way, h], pair_in.at[way, h], pair_s.at[number], pair_r.at[number],
                right if way else left,
            )
            copy.start()
            pair_copies[h, way] = copy

    ring(0)
    x_out[...] = share((1 - x_hi) * 8 + z).astype(BF16)
    swap = remote(x_out, x_in, x_s.at[0], x_r.at[0], x_far)
    swap.start()
    backward(0, 0)
    backward(0, 2)
    ring(1)
    backward(1, 0)
    backward(1, 2)
    ring(2)
    backward(2, 0)
    backward(2, 2)
    ring(3)
    for h in range(HEADS_HERE):
        backward(h, 1)
        dq_ref[:, head(h)] = (dq_acc[h] * INV_ROOT).astype(BF16).T

    for h in range(HEADS_HERE):
        cols = head(h)
        for way in range(2):
            pair_copies[h, way].wait_recv()
        total = own_pair[h] + pair_in[0, h].astype(F32) + pair_in[1, h].astype(F32)
        dk_ref[:, cols] = (total[:, :HEAD_DIM] * INV_ROOT).astype(BF16)
        dv_ref[:, cols] = total[:, HEAD_DIM:].astype(BF16)

    swap.wait_recv()
    total = share(x_hi * 8 + z) + x_in[...].astype(F32)
    for way in range(2):
        for x in range(2):
            number = way * 8 + x * 4 + 3
            pltpu.make_async_copy(ring_out.at[way, x, 3], ring_in.at[way, x, 3], ring_r.at[number]).wait()
            total += ring_in[way, x, 3].astype(F32)
    wg_ref[...] = total.astype(BF16)

    for copy in sent:
        copy.wait_send()


def copy_out(*refs):
    given, out, kept, sem = refs[:4], refs[4:8], refs[8:12], refs[12]
    reads = [pltpu.make_async_copy(given[i], kept[i], sem.at[i]) for i in range(4)]
    writes = [pltpu.make_async_copy(kept[i], out[i], sem.at[4 + i]) for i in range(4)]
    for copy in reads:
        copy.start()
    for read, write in zip(reads, writes, strict=True):
        read.wait()
        write.start()
    for copy in writes:
        copy.wait()


def body(queries, keys, values, out_grad, out_weight, window, counts):
    hbm = pl.BlockSpec(memory_space=pl.ANY)
    vmem = pl.BlockSpec(memory_space=pltpu.VMEM)
    smem = pl.BlockSpec(memory_space=pltpu.SMEM)
    V = pltpu.VMEM
    dma = pltpu.SemaphoreType.DMA
    block = jax.ShapeDtypeStruct((TOK, COLS), BF16)
    scratch = [
        V((TOK, COLS), BF16),
        V((3, HEADS_HERE, TOK, HEAD_DIM), BF16),
        V((3, HEADS_HERE, TOK, HEAD_DIM), BF16),
        V((TOK, COLS), BF16),
        V((COLS, TP * COLS), BF16),
        V((TP, COLS, TOK), BF16),
        V((3, HEADS_HERE, HEAD_DIM, TOK), BF16),
        V((3, HEADS_HERE, HEAD_DIM, TOK), BF16),
        V((HEADS_HERE, 3, 2, SPAN, HALF), BF16),
        V((3, SPAN, HALF), F32),
        V((2, 16, HALF), F32),
        V((COLS, TOK), BF16),
        V((TOK, COLS), BF16),
        V((HEADS_HERE, 1, TOK), F32),
        V((HEADS_HERE, 1, TOK), F32),
        V((COLS, TOK), F32),
        V((COLS, TOK), BF16),
        V((TOK, COLS), BF16),
        V((HEADS_HERE, HEAD_DIM, TOK), F32),
        V((TOK, HALF), F32),
        V((HEADS_HERE, TOK, HALF), F32),
        V((2, HEADS_HERE, TOK, HALF), BF16),
        V((2, HEADS_HERE, TOK, HALF), BF16),
        V((COLS, COLS), F32),
        V((16, STRIP, COLS), F32),
        V((16, STRIP, COLS), BF16),
        V((16, STRIP, COLS), BF16),
        V((2, 2, 4, STRIP, COLS), BF16),
        V((2, 2, 4, STRIP, COLS), BF16),
        V((STRIP, COLS), BF16),
        V((STRIP, COLS), BF16),
        dma((9,)),
        dma((12,)), dma((12,)),
        dma((GATHERS,)), dma((GATHERS,)),
        dma((6,)), dma((6,)),
        dma((8,)), dma((8,)),
        dma((16,)), dma((16,)),
        dma((1,)), dma((1,)),
    ]
    dq, dk, dv, wg = pl.pallas_call(
        kernel,
        out_shape=(block, block, block, jax.ShapeDtypeStruct((STRIP, COLS), BF16)),
        in_specs=[smem, smem, hbm, hbm, hbm, hbm, hbm],
        out_specs=(vmem, vmem, vmem, vmem),
        scratch_shapes=scratch,
        compiler_params=pltpu.CompilerParams(
            collective_id=0, has_side_effects=True, vmem_limit_bytes=56 * 1024 * 1024
        ),
    )(window.T, counts, queries, keys, values, out_grad, out_weight)
    results = (dq, dk, dv, wg)
    dq, dk, dv, wg = pl.pallas_call(
        copy_out,
        out_shape=tuple(jax.ShapeDtypeStruct(r.shape, BF16) for r in results),
        in_specs=[hbm] * 4,
        out_specs=(hbm,) * 4,
        scratch_shapes=[V(r.shape, BF16) for r in results] + [dma((8,))],
    )(*results)
    return dq, dk, dv, wg.T


def solution(mesh):
    in_specs = (
        P("lon", "tp"),
        P("lon", "tp"),
        P("lon", "tp"),
        P("lon", "tp"),
        P("tp", None),
        P(),
        P(),
    )
    out_specs = (P("lon", "tp"), P("lon", "tp"), P("lon", "tp"), P("tp", "lon"))
    return jax.shard_map(body, mesh=mesh, in_specs=in_specs, out_specs=out_specs, check_vma=False)
```

```python
import jax
import jax.numpy as jnp
from jax import lax
from jax.experimental import pallas as pl
from jax.experimental.pallas import tpu as pltpu
from jax.sharding import PartitionSpec as P

MESH = pl.DeviceIdType.MESH
F32 = jnp.float32
BF16 = jnp.bfloat16
HEAD_DIM = 128
TILE = 128
HEADS_HERE = 3
TOK = 512
COLS = HEADS_HERE * HEAD_DIM
SPAN = 3 * TILE
HALF = 2 * TILE
WIN = 9
LON = 32
TP = 8
STRIP = 96
GATHERS = 28
INV_ROOT = HEAD_DIM ** -0.5
LOG2E = 1.4426950408889634
NEG = -1e30

NT = (((1,), (1,)), ((), ()))


def dot(a, b):
    return jnp.dot(a, b, preferred_element_type=F32)


def kernel(
    win_ref, cnt_ref, q_hbm, k_hbm, v_hbm, og_hbm, w_hbm,
    dq_ref, dk_ref, dv_ref, wg_ref,
    q_all, k_all, v_all, og_v, w_v, og_t, k_t, v_t, prob, prob_near, scores, bias, bias_near, top_all,
    att_t, att, inv_sum, delta, do_acc, do_all, pair,
    wg_full, wg_own, core_out, core_in,
    ring_out, ring_in, last_in, x_out, x_in,
    loc_sem, halo_s, halo_r, ag_s, ag_r, ask_s, ask_r, stat_s, stat_r, tell_s, tell_r, core_s, core_r,
    ring_s, ring_r, last_r, x_s, x_r,
):
    lon = lax.axis_index("lon")
    tp = lax.axis_index("tp")
    x_hi = lax.div(lon, 16)
    z = lax.rem(lax.div(lon, 2), 8)
    core = lax.rem(lon, 2)
    y = lax.div(tp, 2)
    x_lo = lax.rem(tp, 2)

    right = {"lon": lax.rem(lon + 1, LON)}
    left = {"lon": lax.rem(lon + LON - 1, LON)}
    twin = {"lon": lon + 1 - 2 * core}
    z_up = {"lon": x_hi * 16 + lax.rem(z + 1, 8) * 2 + core}
    z_down = {"lon": x_hi * 16 + lax.rem(z + 7, 8) * 2 + core}
    z_up2 = {"lon": x_hi * 16 + lax.rem(z + 2, 8) * 2 + core}
    z_down2 = {"lon": x_hi * 16 + lax.rem(z + 6, 8) * 2 + core}
    x_far = {"lon": lax.rem(lon + 16, LON)}
    up_far = {"lon": (1 - x_hi) * 16 + lax.rem(z + 1, 8) * 2 + core}
    down_far = {"lon": (1 - x_hi) * 16 + lax.rem(z + 7, 8) * 2 + core}
    y_p = lax.rem(y + 1, 4)
    y_m = lax.rem(y + 3, 4)
    y_2 = lax.rem(y + 2, 4)
    s_x = y * 2 + 1 - x_lo
    s_p = y_p * 2 + x_lo
    s_m = y_m * 2 + x_lo
    s_2 = y_2 * 2 + x_lo
    s_px = y_p * 2 + 1 - x_lo
    s_mx = y_m * 2 + 1 - x_lo
    s_2x = y_2 * 2 + 1 - x_lo
    to_x, to_p, to_m = {"tp": s_x}, {"tp": s_p}, {"tp": s_m}

    barrier = pltpu.get_barrier_semaphore()
    for other in (right, left, z_up, z_down, z_up2, z_down2, x_far, up_far, down_far, to_x, to_p, to_m):
        pl.semaphore_signal(barrier, inc=1, device_id=other, device_id_type=MESH)

    def head(h):
        return slice(h * HEAD_DIM, (h + 1) * HEAD_DIM)

    local_og = pltpu.make_async_copy(og_hbm, og_v, loc_sem.at[0])
    local_kv = [
        pltpu.make_async_copy(src.at[:, head(h)], dst.at[1, h], loc_sem.at[1 + 3 * h + i])
        for h in range(HEADS_HERE)
        for i, (src, dst) in enumerate(((k_hbm, k_all), (v_hbm, v_all), (q_hbm, q_all)))
    ]
    local_w = pltpu.make_async_copy(w_hbm, w_v, loc_sem.at[10])
    for copy in (local_og, *local_kv, local_w):
        copy.start()

    sent = []

    def remote(src, dst, send, recv, to):
        copy = pltpu.make_async_remote_copy(
            src_ref=src, dst_ref=dst, send_sem=send, recv_sem=recv, device_id=to, device_id_type=MESH
        )
        sent.append(copy)
        return copy

    count = iter(range(GATHERS))

    def gather(slot, quarter, to):
        block = og_t.at[slot, pl.ds(quarter * STRIP, STRIP)]
        number = next(count)
        return remote(block, block, ag_s.at[number], ag_r.at[number], to)

    x0 = {i: gather(tp, i, to_x) for i in (0, 1, 2, 3)}
    p0 = {i: gather(tp, i, to_p) for i in (2, 3, 0, 1)}
    m0 = {i: gather(tp, i, to_m) for i in (0, 1, 2, 3)}
    p1 = {i: gather(s_m, i, to_p) for i in (2, 3)}
    m1 = {i: gather(s_p, i, to_m) for i in (0, 1)}
    p2 = {i: gather(s_x, i, to_p) for i in (2, 3, 1)}
    m2 = {i: gather(s_x, i, to_m) for i in (0, 1, 2)}
    x1 = {3: gather(s_p, 3, to_x)}
    x2 = {0: gather(s_m, 0, to_x)}
    p3 = {i: gather(s_mx, i, to_p) for i in (2, 3)}
    m3 = {i: gather(s_px, i, to_m) for i in (0, 1)}

    halo = []
    for h in range(HEADS_HERE):
        part = []
        for i, ref in enumerate((k_all, v_all)):
            for j, to in enumerate((right, left)):
                number = h * 4 + i * 2 + j
                part.append(
                    remote(ref.at[1, h], ref.at[2 * j, h], halo_s.at[number], halo_r.at[number], to)
                )
        halo.append(part)
    ways = (right, left)
    ask = [
        [remote(q_all.at[1, h], q_all.at[2 * j, h], ask_s.at[2 * h + j], ask_r.at[2 * h + j], ways[j]) for j in range(2)]
        for h in range(HEADS_HERE)
    ]

    local_og.wait()
    og_t[tp] = og_v[...].T
    for copy in local_kv:
        copy.wait()
    pl.semaphore_wait(barrier, 12)
    for i, (a, b, c) in enumerate(zip(x0.values(), p0.values(), m0.values(), strict=True)):
        a.start()
        b.start()
        c.start()

    around = (lax.rem(lon, 16) == 15, lax.rem(lon, 16) == 0)

    def send_halo(late):
        for j in range(2):
            @pl.when(around[j] if late else jnp.logical_not(around[j]))
            def _():
                for h in range(HEADS_HERE):
                    halo[h][j].start()
                    halo[h][2 + j].start()
                for h in range(HEADS_HERE):
                    ask[h][j].start()

    send_halo(False)

    lane = lax.broadcasted_iota(jnp.int32, (1, HALF), 1)
    words = []
    for t in range(4):
        tile = lon * 4 + t
        word = jnp.int32(0)
        for slot in range(WIN):
            other = win_ref[slot, tile]
            place = lax.rem(lax.div(other, 4) + (LON + 1) - lon, LON) * 4 + lax.rem(other, 4)
            live = (slot < cnt_ref[tile]).astype(jnp.int32)
            word = word | lax.shift_left(live, place)
        words.append(word)
    for a in range(2):
        for n in range(3):
            for r in range(3):
                code = n * 4 + a + r
                fill = [
                    jnp.where((lax.shift_right_logical(words[2 * a + i], jnp.int32(code)) & 1) == 1, 0.0, NEG)
                    for i in range(2)
                ]
                bias[a, n * 3 + r : n * 3 + r + 1, :] = jnp.where(lane < TILE, fill[0], fill[1]).astype(F32)

    for i, stripe in enumerate((lax.rem(lon + LON - 1, LON), lax.rem(lon + 1, LON))):
        words = []
        for t in range(4):
            tile = stripe * 4 + t
            word = jnp.int32(0)
            for slot in range(WIN):
                other = win_ref[slot, tile]
                live = ((slot < cnt_ref[tile]) & (lax.div(other, 4) == lon)).astype(jnp.int32)
                word = word | lax.shift_left(live, lax.rem(other, 4))
            words.append(word)
        for a in range(2):
            for r in range(3):
                fill = [
                    jnp.where((lax.shift_right_logical(words[2 * a + i2], jnp.int32(a + r)) & 1) == 1, 0.0, NEG)
                    for i2 in range(2)
                ]
                bias_near[i, a, r : r + 1, :] = jnp.where(lane < TILE, fill[0], fill[1]).astype(F32)

    for h in range(HEADS_HERE):
        k_t[1, h] = k_all[1, h].T
        v_t[1, h] = v_all[1, h].T

    def forward(h, a):
        cols = head(h)
        here = slice(a * HALF, (a + 1) * HALF)
        keys = slice(a * TILE, a * TILE + SPAN)
        q = q_all[1, h, here, :]
        top = None
        for n in range(3):
            s = lax.dot_general(k_all[n, h, keys, :], q, NT, preferred_element_type=F32)
            s = s.reshape(3, TILE, HALF) * (INV_ROOT * LOG2E) + bias[a, n * 3 : n * 3 + 3][:, None, :]
            s = s.reshape(SPAN, HALF)
            scores[n] = s
            peak = jnp.max(s, axis=0, keepdims=True)
            top = peak if top is None else jnp.maximum(top, peak)
        total = jnp.zeros((1, HALF), F32)
        out = jnp.zeros((HEAD_DIM, HALF), F32)
        for n in range(3):
            e = jnp.exp2(scores[n] - top)
            total += jnp.sum(e, axis=0, keepdims=True)
            low = e.astype(BF16)
            prob[h, n, a] = low
            out += dot(v_t[n, h, :, keys], low)
        top_all[1, h : h + 1, here] = top
        inverse = 1.0 / total
        inv_sum[h, :, here] = inverse
        att_t[cols, here] = (out * inverse).astype(BF16)

    def passed(before, after):
        for copy in before:
            copy.wait_recv()
        for copy in after:
            copy.start()

    passed((p0[2], p0[3], m0[0], m0[1]), (*p1.values(), *m1.values()))
    passed((x0[0], x0[1], x0[2]), (p2[2], m2[0], m2[1]))
    passed((x0[3],), (p2[3], m2[2], p2[1]))
    passed((m0[2], m0[3], p0[0], p0[1]), (x1[3], x2[0]))
    send_halo(True)

    for h in range(HEADS_HERE):
        for copy in halo[h]:
            copy.wait_recv()
        for n in (0, 2):
            v_t[n, h] = v_all[n, h].T
        forward(h, 0)
        forward(h, 1)
        if h < 2:
            passed((p2[2 + h], m2[h]), (p3[2 + h], m3[h]))
    tops = [
        remote(top_all.at[1], top_all.at[2 * j], stat_s.at[j], stat_r.at[j], ways[j]) for j in range(2)
    ]
    for copy in tops:
        copy.start()
    att[...] = att_t[...].T
    for h in range(HEADS_HERE):
        for n in (0, 2):
            k_t[n, h] = k_all[n, h].T

    def recall(i, h):
        for a in range(2):
            here = slice(a * HALF, (a + 1) * HALF)
            keys = slice(a * TILE, a * TILE + SPAN)
            s = lax.dot_general(
                k_all[1, h, keys, :], q_all[2 * i, h, here, :], NT, preferred_element_type=F32
            ).reshape(3, TILE, HALF)
            less = bias_near[i, a, 0:3] - top_all[2 * i, h : h + 1, here]
            e = jnp.exp2(s * (INV_ROOT * LOG2E) + less[:, None, :])
            prob_near[i, h, a] = e.reshape(SPAN, HALF).astype(BF16)

    core_copies = []

    def use_piece(order, piece):
        block = og_t[piece]
        part = dot(w_v[:, pl.ds(pl.multiple_of(piece * COLS, COLS), COLS)], block)
        if order == 0:
            do_acc[...] = part
        else:
            do_acc[...] += part
        wg_full[...] = dot(block, att[...])
        for j in range(2):
            wg_own[piece * 2 + j] = wg_full[pl.ds(pl.multiple_of((2 * j + core) * STRIP, STRIP), STRIP)]
            core_out[piece * 2 + j] = wg_full[
                pl.ds(pl.multiple_of((2 * j + 1 - core) * STRIP, STRIP), STRIP)
            ].astype(BF16)
        both = pl.ds(piece * 2, 2)
        copy = remote(core_out.at[both], core_in.at[both], core_s.at[order], core_r.at[order], twin)
        copy.start()
        core_copies.append(copy)

    def share(block):
        return wg_own[block] + core_in[block].astype(F32)

    chains = {}

    def chain(wave, way, s):
        step = lax.rem(z + (4 - s if way == 0 else 4 + s), 8)
        odd = lax.rem(lax.div(step, 4) + y, 2)
        plane = (1 - odd) * lax.div(y, 2) + odd * lax.div(y_p, 2)
        if wave == 1:
            plane = 1 - plane
        value = share(plane * 8 + step)
        for before in ((), (), (0, 1) if way == wave else (1,), (2,))[s]:
            chains[wave, way, before].wait_recv()
            value += ring_in[wave, way, before].astype(F32)
        ring_out[wave, way, s] = value.astype(BF16)
        number = wave * 8 + way * 4 + s
        if s < 3:
            copy = remote(
                ring_out.at[wave, way, s], ring_in.at[wave, way, s], ring_s.at[number], ring_r.at[number],
                ((z_up2, z_down2) if s == 0 else (z_up, z_down))[way],
            )
        else:
            copy = remote(
                ring_out.at[wave, way, s], last_in.at[way, x_hi], ring_s.at[number], last_r.at[way * 2 + x_hi],
                {"lon": plane * 16 + lax.rem(z + (7 if way else 1), 8) * 2 + core},
            )
        copy.start()
        chains[wave, way, s] = copy

    def ring(wave, point):
        if point == 0:
            for copy in core_copies[4 * wave : 4 * wave + 4]:
                copy.wait_recv()
            chain(wave, wave, 0)
        for way in range(2):
            chain(wave, way, point + 1)

    local_w.wait()
    use_piece(0, tp)
    use_piece(1, s_x)
    use_piece(2, s_p)
    passed((x1[3], m2[2]), ())
    use_piece(3, s_px)
    use_piece(4, s_m)
    ring(0, 0)
    passed((*p1.values(), *m1.values()), ())
    use_piece(5, s_2)
    passed((x2[0], p2[1]), ())
    use_piece(6, s_mx)
    passed((*p3.values(), *m3.values()), ())
    use_piece(7, s_2x)

    ring(1, 0)
    x_out[...] = share((1 - x_hi) * 8 + z).astype(BF16)
    swap = remote(x_out, x_in, x_s.at[0], x_r.at[0], x_far)
    swap.start()

    tell = []
    for h in range(HEADS_HERE):
        rows = head(h)
        scaled = (do_acc[rows] * inv_sum[h]).astype(BF16)
        do_all[1, h] = scaled
        delta[1, h : h + 1, :] = jnp.sum(scaled.astype(F32) * att_t[rows].astype(F32), axis=0, keepdims=True)
        for j in range(2):
            copy = remote(do_all.at[1, h], do_all.at[2 * j, h], tell_s.at[2 * h + j], tell_r.at[2 * h + j], ways[j])
            copy.start()
            tell.append(copy)
    deltas = [
        remote(delta.at[1], delta.at[2 * j], stat_s.at[2 + j], stat_r.at[2 + j], ways[j]) for j in range(2)
    ]
    for copy in deltas:
        copy.start()

    def spread(e, h, n, a, low, keep):
        here = slice(a * HALF, (a + 1) * HALF)
        keys = slice(a * TILE, a * TILE + SPAN)
        value = v_all[e, h, keys, :]
        grad = do_all[n, h, :, here]
        ds = (low.astype(F32) * (dot(value, grad) - delta[n, h : h + 1, here])).astype(BF16)
        if e == 1:
            dkey = dot(ds, q_all[n, h, here, :])
            dval = lax.dot_general(low, grad, NT, preferred_element_type=F32)
            if keep:
                pair[h, keys, 0:HEAD_DIM] += dkey
                pair[h, keys, HEAD_DIM:] += dval
            elif a == 0:
                pair[h, keys, 0:HEAD_DIM] = dkey
                pair[h, keys, HEAD_DIM:] = dval
            else:
                pair[h, TILE:SPAN, 0:HEAD_DIM] += dkey[:HALF]
                pair[h, TILE:SPAN, HEAD_DIM:] += dval[:HALF]
                pair[h, SPAN:, 0:HEAD_DIM] = dkey[HALF:]
                pair[h, SPAN:, HEAD_DIM:] = dval[HALF:]
        return ds

    def own_queries(h):
        for a in range(2):
            keys = slice(a * TILE, a * TILE + SPAN)
            total = None
            for n in range(3):
                ds = spread(n, h, 1, a, prob[h, n, a], False)
                part = dot(k_t[n, h, :, keys], ds)
                total = part if total is None else total + part
            dq_ref[a * HALF : (a + 1) * HALF, head(h)] = (total * INV_ROOT).astype(BF16).T

    def near_queries(h):
        for i in range(2):
            tell[2 * h + i].wait_recv()
            for a in range(2):
                spread(1, h, 2 * i, a, prob_near[i, h, a], True)
        dk_ref[:, head(h)] = (pair[h, :, 0:HEAD_DIM] * INV_ROOT).astype(BF16)
        dv_ref[:, head(h)] = pair[h, :, HEAD_DIM:].astype(BF16)

    ring(0, 1)
    for copy in tops:
        copy.wait_recv()
    for h in range(HEADS_HERE):
        for i in range(2):
            ask[h][i].wait_recv()
            recall(i, h)
    own_queries(0)
    ring(1, 1)
    ring(0, 2)
    own_queries(1)
    own_queries(2)
    ring(1, 2)
    for copy in deltas:
        copy.wait_recv()
    near_queries(0)
    near_queries(1)
    near_queries(2)

    swap.wait_recv()
    total = share(x_hi * 8 + z) + x_in[...].astype(F32)
    for way in range(2):
        for x in range(2):
            block = last_in.at[way, x]
            pltpu.make_async_copy(x_out, block, last_r.at[way * 2 + x]).wait()
            total += last_in[way, x].astype(F32)
    wg_ref[...] = total.astype(BF16)

    for copy in sent:
        copy.wait_send()


def copy_out(*refs):
    given, out, kept, sem = refs[:4], refs[4:8], refs[8:12], refs[12]
    reads = [pltpu.make_async_copy(given[i], kept[i], sem.at[i]) for i in range(4)]
    writes = [pltpu.make_async_copy(kept[i], out[i], sem.at[4 + i]) for i in range(4)]
    for copy in reads:
        copy.start()
    for read, write in zip(reads, writes, strict=True):
        read.wait()
        write.start()
    for copy in writes:
        copy.wait()


def body(queries, keys, values, out_grad, out_weight, window, counts):
    hbm = pl.BlockSpec(memory_space=pl.ANY)
    vmem = pl.BlockSpec(memory_space=pltpu.VMEM)
    smem = pl.BlockSpec(memory_space=pltpu.SMEM)
    V = pltpu.VMEM
    dma = pltpu.SemaphoreType.DMA
    block = jax.ShapeDtypeStruct((TOK, COLS), BF16)
    scratch = [
        V((3, HEADS_HERE, TOK, HEAD_DIM), BF16),
        V((3, HEADS_HERE, TOK, HEAD_DIM), BF16),
        V((3, HEADS_HERE, TOK, HEAD_DIM), BF16),
        V((TOK, COLS), BF16),
        V((COLS, TP * COLS), BF16),
        V((TP, COLS, TOK), BF16),
        V((3, HEADS_HERE, HEAD_DIM, TOK), BF16),
        V((3, HEADS_HERE, HEAD_DIM, TOK), BF16),
        V((HEADS_HERE, 3, 2, SPAN, HALF), BF16),
        V((2, HEADS_HERE, 2, SPAN, HALF), BF16),
        V((3, SPAN, HALF), F32),
        V((2, 16, HALF), F32),
        V((2, 2, 8, HALF), F32),
        V((3, 8, TOK), F32),
        V((COLS, TOK), BF16),
        V((TOK, COLS), BF16),
        V((HEADS_HERE, 1, TOK), F32),
        V((3, 8, TOK), F32),
        V((COLS, TOK), F32),
        V((3, HEADS_HERE, HEAD_DIM, TOK), BF16),
        V((HEADS_HERE, TOK, HALF), F32),
        V((COLS, COLS), F32),
        V((16, STRIP, COLS), F32),
        V((16, STRIP, COLS), BF16),
        V((16, STRIP, COLS), BF16),
        V((2, 2, 4, STRIP, COLS), BF16),
        V((2, 2, 4, STRIP, COLS), BF16),
        V((2, 2, STRIP, COLS), BF16),
        V((STRIP, COLS), BF16),
        V((STRIP, COLS), BF16),
        dma((11,)),
        dma((12,)), dma((12,)),
        dma((GATHERS,)), dma((GATHERS,)),
        dma((6,)), dma((6,)),
        dma((4,)), dma((4,)),
        dma((6,)), dma((6,)),
        dma((8,)), dma((8,)),
        dma((16,)), dma((16,)),
        dma((4,)),
        dma((1,)), dma((1,)),
    ]
    dq, dk, dv, wg = pl.pallas_call(
        kernel,
        out_shape=(block, block, block, jax.ShapeDtypeStruct((STRIP, COLS), BF16)),
        in_specs=[smem, smem, hbm, hbm, hbm, hbm, hbm],
        out_specs=(vmem, vmem, vmem, vmem),
        scratch_shapes=scratch,
        compiler_params=pltpu.CompilerParams(
            collective_id=0, has_side_effects=True, vmem_limit_bytes=56 * 1024 * 1024
        ),
    )(window.T, counts, queries, keys, values, out_grad, out_weight)
    results = (dq, dk, dv, wg)
    dq, dk, dv, wg = pl.pallas_call(
        copy_out,
        out_shape=tuple(jax.ShapeDtypeStruct(r.shape, BF16) for r in results),
        in_specs=[hbm] * 4,
        out_specs=(hbm,) * 4,
        scratch_shapes=[V(r.shape, BF16) for r in results] + [dma((8,))],
    )(*results)
    return dq, dk, dv, wg.T


def solution(mesh):
    in_specs = (
        P("lon", "tp"),
        P("lon", "tp"),
        P("lon", "tp"),
        P("lon", "tp"),
        P("tp", None),
        P(),
        P(),
    )
    out_specs = (P("lon", "tp"), P("lon", "tp"), P("lon", "tp"), P("tp", "lon"))
    return jax.shard_map(body, mesh=mesh, in_specs=in_specs, out_specs=out_specs, check_vma=False)
```

```python
import jax
import jax.numpy as jnp
from jax import lax
from jax.experimental import pallas as pl
from jax.experimental.pallas import tpu as pltpu
from jax.sharding import PartitionSpec as P

MESH = pl.DeviceIdType.MESH
F32 = jnp.float32
BF16 = jnp.bfloat16
HEAD_DIM = 128
TILE = 128
HEADS_HERE = 3
TOK = 512
COLS = HEADS_HERE * HEAD_DIM
SPAN = 3 * TILE
HALF = 2 * TILE
WIN = 9
LON = 32
TP = 8
STRIP = 96
GATHERS = 28
INV_ROOT = HEAD_DIM ** -0.5
LOG2E = 1.4426950408889634
NEG = -1e30

NT = (((1,), (1,)), ((), ()))


def dot(a, b):
    return jnp.dot(a, b, preferred_element_type=F32)


def kernel(
    win_ref, cnt_ref, q_hbm, k_hbm, v_hbm, og_hbm, w_hbm,
    dq_ref, dk_ref, dv_ref, wg_ref,
    q_all, k_all, v_all, og_v, w_v, og_t, k_t, v_t, prob, prob_near, scores, bias, bias_near, top_all,
    att_t, att, inv_sum, delta, do_acc, do_all, pair,
    wg_full, wg_own, core_out, core_in,
    ring_out, ring_in, last_in, x_out, x_in,
    loc_sem, halo_s, halo_r, ag_s, ag_r, ask_s, ask_r, stat_s, stat_r, tell_s, tell_r, core_s, core_r,
    ring_s, ring_r, last_r, x_s, x_r,
):
    lon = lax.axis_index("lon")
    tp = lax.axis_index("tp")
    x_hi = lax.div(lon, 16)
    z = lax.rem(lax.div(lon, 2), 8)
    core = lax.rem(lon, 2)
    y = lax.div(tp, 2)
    x_lo = lax.rem(tp, 2)

    right = {"lon": lax.rem(lon + 1, LON)}
    left = {"lon": lax.rem(lon + LON - 1, LON)}
    twin = {"lon": lon + 1 - 2 * core}
    z_up = {"lon": x_hi * 16 + lax.rem(z + 1, 8) * 2 + core}
    z_down = {"lon": x_hi * 16 + lax.rem(z + 7, 8) * 2 + core}
    z_up2 = {"lon": x_hi * 16 + lax.rem(z + 2, 8) * 2 + core}
    z_down2 = {"lon": x_hi * 16 + lax.rem(z + 6, 8) * 2 + core}
    x_far = {"lon": lax.rem(lon + 16, LON)}
    up_far = {"lon": (1 - x_hi) * 16 + lax.rem(z + 1, 8) * 2 + core}
    down_far = {"lon": (1 - x_hi) * 16 + lax.rem(z + 7, 8) * 2 + core}
    y_p = lax.rem(y + 1, 4)
    y_m = lax.rem(y + 3, 4)
    y_2 = lax.rem(y + 2, 4)
    s_x = y * 2 + 1 - x_lo
    s_p = y_p * 2 + x_lo
    s_m = y_m * 2 + x_lo
    s_2 = y_2 * 2 + x_lo
    s_px = y_p * 2 + 1 - x_lo
    s_mx = y_m * 2 + 1 - x_lo
    s_2x = y_2 * 2 + 1 - x_lo
    to_x, to_p, to_m = {"tp": s_x}, {"tp": s_p}, {"tp": s_m}

    barrier = pltpu.get_barrier_semaphore()
    for other in (right, left, z_up, z_down, z_up2, z_down2, x_far, up_far, down_far, to_x, to_p, to_m):
        pl.semaphore_signal(barrier, inc=1, device_id=other, device_id_type=MESH)

    def head(h):
        return slice(h * HEAD_DIM, (h + 1) * HEAD_DIM)

    local_og = pltpu.make_async_copy(og_hbm, og_v, loc_sem.at[0])
    local_kv = [
        pltpu.make_async_copy(src.at[:, head(h)], dst.at[1, h], loc_sem.at[1 + 3 * h + i])
        for h in range(HEADS_HERE)
        for i, (src, dst) in enumerate(((k_hbm, k_all), (v_hbm, v_all), (q_hbm, q_all)))
    ]
    local_w = pltpu.make_async_copy(w_hbm, w_v, loc_sem.at[10])
    for copy in (local_og, *local_kv, local_w):
        copy.start()

    sent = []

    def remote(src, dst, send, recv, to):
        copy = pltpu.make_async_remote_copy(
            src_ref=src, dst_ref=dst, send_sem=send, recv_sem=recv, device_id=to, device_id_type=MESH
        )
        sent.append(copy)
        return copy

    count = iter(range(GATHERS))

    def gather(slot, quarter, to):
        block = og_t.at[slot, pl.ds(quarter * STRIP, STRIP)]
        number = next(count)
        return remote(block, block, ag_s.at[number], ag_r.at[number], to)

    x0 = {i: gather(tp, i, to_x) for i in (0, 1, 2, 3)}
    p0 = {i: gather(tp, i, to_p) for i in (2, 3, 0, 1)}
    m0 = {i: gather(tp, i, to_m) for i in (0, 1, 2, 3)}
    p1 = {i: gather(s_m, i, to_p) for i in (2, 3)}
    m1 = {i: gather(s_p, i, to_m) for i in (0, 1)}
    p2 = {i: gather(s_x, i, to_p) for i in (2, 3, 1)}
    m2 = {i: gather(s_x, i, to_m) for i in (0, 1, 2)}
    x1 = {3: gather(s_p, 3, to_x)}
    x2 = {0: gather(s_m, 0, to_x)}
    p3 = {i: gather(s_mx, i, to_p) for i in (2, 3)}
    m3 = {i: gather(s_px, i, to_m) for i in (0, 1)}

    halo = []
    for h in range(HEADS_HERE):
        part = []
        for i, ref in enumerate((k_all, v_all)):
            for j, to in enumerate((right, left)):
                number = h * 4 + i * 2 + j
                part.append(
                    remote(ref.at[1, h], ref.at[2 * j, h], halo_s.at[number], halo_r.at[number], to)
                )
        halo.append(part)
    ways = (right, left)
    ask = [
        [remote(q_all.at[1, h], q_all.at[2 * j, h], ask_s.at[2 * h + j], ask_r.at[2 * h + j], ways[j]) for j in range(2)]
        for h in range(HEADS_HERE)
    ]

    local_og.wait()
    og_t[tp] = og_v[...].T
    for copy in local_kv:
        copy.wait()
    pl.semaphore_wait(barrier, 12)
    for i, (a, b, c) in enumerate(zip(x0.values(), p0.values(), m0.values(), strict=True)):
        a.start()
        b.start()
        c.start()

    around = (lax.rem(lon, 16) == 15, lax.rem(lon, 16) == 0)

    def send_halo(late):
        for j in range(2):
            @pl.when(around[j] if late else jnp.logical_not(around[j]))
            def _():
                for h in range(HEADS_HERE):
                    halo[h][j].start()
                    halo[h][2 + j].start()
                for h in range(HEADS_HERE):
                    ask[h][j].start()

    send_halo(False)

    lane = lax.broadcasted_iota(jnp.int32, (1, HALF), 1)
    words = []
    for t in range(4):
        tile = lon * 4 + t
        word = jnp.int32(0)
        for slot in range(WIN):
            other = win_ref[slot, tile]
            place = lax.rem(lax.div(other, 4) + (LON + 1) - lon, LON) * 4 + lax.rem(other, 4)
            live = (slot < cnt_ref[tile]).astype(jnp.int32)
            word = word | lax.shift_left(live, place)
        words.append(word)
    for a in range(2):
        for n in range(3):
            for r in range(3):
                code = n * 4 + a + r
                fill = [
                    jnp.where((lax.shift_right_logical(words[2 * a + i], jnp.int32(code)) & 1) == 1, 0.0, NEG)
                    for i in range(2)
                ]
                bias[a, n * 3 + r : n * 3 + r + 1, :] = jnp.where(lane < TILE, fill[0], fill[1]).astype(F32)

    for i, stripe in enumerate((lax.rem(lon + LON - 1, LON), lax.rem(lon + 1, LON))):
        words = []
        for t in range(4):
            tile = stripe * 4 + t
            word = jnp.int32(0)
            for slot in range(WIN):
                other = win_ref[slot, tile]
                live = ((slot < cnt_ref[tile]) & (lax.div(other, 4) == lon)).astype(jnp.int32)
                word = word | lax.shift_left(live, lax.rem(other, 4))
            words.append(word)
        for a in range(2):
            for r in range(3):
                fill = [
                    jnp.where((lax.shift_right_logical(words[2 * a + i2], jnp.int32(a + r)) & 1) == 1, 0.0, NEG)
                    for i2 in range(2)
                ]
                bias_near[i, a, r : r + 1, :] = jnp.where(lane < TILE, fill[0], fill[1]).astype(F32)

    for h in range(HEADS_HERE):
        k_t[1, h] = k_all[1, h].T
        v_t[1, h] = v_all[1, h].T

    def forward(h, a):
        cols = head(h)
        here = slice(a * HALF, (a + 1) * HALF)
        keys = slice(a * TILE, a * TILE + SPAN)
        q = q_all[1, h, here, :]
        top = None
        for n in range(3):
            s = lax.dot_general(k_all[n, h, keys, :], q, NT, preferred_element_type=F32)
            s = s.reshape(3, TILE, HALF) * (INV_ROOT * LOG2E) + bias[a, n * 3 : n * 3 + 3][:, None, :]
            s = s.reshape(SPAN, HALF)
            scores[n] = s
            peak = jnp.max(s, axis=0, keepdims=True)
            top = peak if top is None else jnp.maximum(top, peak)
        total = jnp.zeros((1, HALF), F32)
        out = jnp.zeros((HEAD_DIM, HALF), F32)
        for n in range(3):
            e = jnp.exp2(scores[n] - top)
            total += jnp.sum(e, axis=0, keepdims=True)
            low = e.astype(BF16)
            prob[h, n, a] = low
            out += dot(v_t[n, h, :, keys], low)
        top_all[1, h : h + 1, here] = top
        inverse = 1.0 / total
        inv_sum[h, :, here] = inverse
        att_t[cols, here] = (out * inverse).astype(BF16)

    def passed(before, after):
        for copy in before:
            copy.wait_recv()
        for copy in after:
            copy.start()

    passed((p0[2], p0[3], m0[0], m0[1]), (*p1.values(), *m1.values()))
    passed((x0[0], x0[1], x0[2]), (p2[2], m2[0], m2[1]))
    passed((x0[3],), (p2[3], m2[2], p2[1]))
    passed((m0[2], m0[3], p0[0], p0[1]), (x1[3], x2[0]))
    send_halo(True)

    for h in range(HEADS_HERE):
        for copy in halo[h]:
            copy.wait_recv()
        for n in (0, 2):
            v_t[n, h] = v_all[n, h].T
        forward(h, 0)
        forward(h, 1)
        if h < 2:
            passed((p2[2 + h], m2[h]), (p3[2 + h], m3[h]))
    tops = [
        remote(top_all.at[1], top_all.at[2 * j], stat_s.at[j], stat_r.at[j], ways[j]) for j in range(2)
    ]
    for copy in tops:
        copy.start()
    att[...] = att_t[...].T
    for h in range(HEADS_HERE):
        for n in (0, 2):
            k_t[n, h] = k_all[n, h].T

    def recall(i, h):
        for a in range(2):
            here = slice(a * HALF, (a + 1) * HALF)
            keys = slice(a * TILE, a * TILE + SPAN)
            s = lax.dot_general(
                k_all[1, h, keys, :], q_all[2 * i, h, here, :], NT, preferred_element_type=F32
            ).reshape(3, TILE, HALF)
            less = bias_near[i, a, 0:3] - top_all[2 * i, h : h + 1, here]
            e = jnp.exp2(s * (INV_ROOT * LOG2E) + less[:, None, :])
            prob_near[i, h, a] = e.reshape(SPAN, HALF).astype(BF16)

    core_copies = []

    def use_piece(order, piece):
        block = og_t[piece]
        part = dot(w_v[:, pl.ds(pl.multiple_of(piece * COLS, COLS), COLS)], block)
        if order == 0:
            do_acc[...] = part
        else:
            do_acc[...] += part
        wg_full[...] = dot(block, att[...])
        for j in range(2):
            wg_own[piece * 2 + j] = wg_full[pl.ds(pl.multiple_of((2 * j + core) * STRIP, STRIP), STRIP)]
            core_out[piece * 2 + j] = wg_full[
                pl.ds(pl.multiple_of((2 * j + 1 - core) * STRIP, STRIP), STRIP)
            ].astype(BF16)
        both = pl.ds(piece * 2, 2)
        copy = remote(core_out.at[both], core_in.at[both], core_s.at[order], core_r.at[order], twin)
        copy.start()
        core_copies.append(copy)

    def share(block):
        return wg_own[block] + core_in[block].astype(F32)

    chains = {}

    def chain(wave, way, s):
        step = lax.rem(z + (4 - s if way == 0 else 4 + s), 8)
        odd = lax.rem(lax.div(step, 4) + y, 2)
        plane = (1 - odd) * lax.div(y, 2) + odd * lax.div(y_p, 2)
        if wave == 1:
            plane = 1 - plane
        value = share(plane * 8 + step)
        for before in ((), (), (0, 1) if way == wave else (1,), (2,))[s]:
            chains[wave, way, before].wait_recv()
            value += ring_in[wave, way, before].astype(F32)
        ring_out[wave, way, s] = value.astype(BF16)
        number = wave * 8 + way * 4 + s
        if s < 3:
            copy = remote(
                ring_out.at[wave, way, s], ring_in.at[wave, way, s], ring_s.at[number], ring_r.at[number],
                ((z_up2, z_down2) if s == 0 else (z_up, z_down))[way],
            )
        else:
            copy = remote(
                ring_out.at[wave, way, s], last_in.at[way, x_hi], ring_s.at[number], last_r.at[way * 2 + x_hi],
                {"lon": plane * 16 + lax.rem(z + (7 if way else 1), 8) * 2 + core},
            )
        copy.start()
        chains[wave, way, s] = copy

    def ring(wave, point):
        if point == 0:
            for copy in core_copies[4 * wave : 4 * wave + 4]:
                copy.wait_recv()
            chain(wave, wave, 0)
        for way in range(2):
            chain(wave, way, point + 1)

    local_w.wait()
    use_piece(0, tp)
    use_piece(1, s_x)
    use_piece(2, s_p)
    passed((x1[3], m2[2]), ())
    use_piece(3, s_px)
    use_piece(4, s_m)
    ring(0, 0)
    passed((*p1.values(), *m1.values()), ())
    use_piece(5, s_2)
    passed((x2[0], p2[1]), ())
    use_piece(6, s_mx)
    passed((*p3.values(), *m3.values()), ())
    use_piece(7, s_2x)

    ring(1, 0)
    x_out[...] = share((1 - x_hi) * 8 + z).astype(BF16)
    swap = remote(x_out, x_in, x_s.at[0], x_r.at[0], x_far)
    swap.start()

    tell = []
    for h in range(HEADS_HERE):
        rows = head(h)
        scaled = (do_acc[rows] * inv_sum[h]).astype(BF16)
        do_all[1, h] = scaled
        delta[1, h : h + 1, :] = jnp.sum(scaled.astype(F32) * att_t[rows].astype(F32), axis=0, keepdims=True)
        for j in range(2):
            copy = remote(do_all.at[1, h], do_all.at[2 * j, h], tell_s.at[2 * h + j], tell_r.at[2 * h + j], ways[j])
            copy.start()
            tell.append(copy)
    deltas = [
        remote(delta.at[1], delta.at[2 * j], stat_s.at[2 + j], stat_r.at[2 + j], ways[j]) for j in range(2)
    ]
    for copy in deltas:
        copy.start()

    def spread(e, h, n, a, low, keep):
        here = slice(a * HALF, (a + 1) * HALF)
        keys = slice(a * TILE, a * TILE + SPAN)
        value = v_all[e, h, keys, :]
        grad = do_all[n, h, :, here]
        ds = (low.astype(F32) * (dot(value, grad) - delta[n, h : h + 1, here])).astype(BF16)
        if e == 1:
            dkey = dot(ds, q_all[n, h, here, :])
            dval = lax.dot_general(low, grad, NT, preferred_element_type=F32)
            if keep:
                pair[h, keys, 0:HEAD_DIM] += dkey
                pair[h, keys, HEAD_DIM:] += dval
            elif a == 0:
                pair[h, keys, 0:HEAD_DIM] = dkey
                pair[h, keys, HEAD_DIM:] = dval
            else:
                pair[h, TILE:SPAN, 0:HEAD_DIM] += dkey[:HALF]
                pair[h, TILE:SPAN, HEAD_DIM:] += dval[:HALF]
                pair[h, SPAN:, 0:HEAD_DIM] = dkey[HALF:]
                pair[h, SPAN:, HEAD_DIM:] = dval[HALF:]
        return ds

    def own_queries(h):
        for a in range(2):
            keys = slice(a * TILE, a * TILE + SPAN)
            total = None
            for n in range(3):
                ds = spread(n, h, 1, a, prob[h, n, a], False)
                part = dot(k_t[n, h, :, keys], ds)
                total = part if total is None else total + part
            dq_ref[a * HALF : (a + 1) * HALF, head(h)] = (total * INV_ROOT).astype(BF16).T

    def near_queries(h):
        for i in range(2):
            tell[2 * h + i].wait_recv()
            for a in range(2):
                spread(1, h, 2 * i, a, prob_near[i, h, a], True)
        dk_ref[:, head(h)] = (pair[h, :, 0:HEAD_DIM] * INV_ROOT).astype(BF16)
        dv_ref[:, head(h)] = pair[h, :, HEAD_DIM:].astype(BF16)

    ring(0, 1)
    for copy in tops:
        copy.wait_recv()
    for h in range(HEADS_HERE):
        for i in range(2):
            ask[h][i].wait_recv()
            recall(i, h)
    own_queries(0)
    ring(1, 1)
    ring(0, 2)
    own_queries(1)
    ring(1, 2)
    own_queries(2)
    for copy in deltas:
        copy.wait_recv()
    near_queries(0)
    near_queries(1)
    near_queries(2)

    swap.wait_recv()
    total = share(x_hi * 8 + z) + x_in[...].astype(F32)
    for way in range(2):
        for x in range(2):
            block = last_in.at[way, x]
            pltpu.make_async_copy(x_out, block, last_r.at[way * 2 + x]).wait()
            total += last_in[way, x].astype(F32)
    wg_ref[...] = total.astype(BF16)

    for copy in sent:
        copy.wait_send()


def copy_out(*refs):
    given, out, kept, sem = refs[:4], refs[4:8], refs[8:12], refs[12]
    reads = [pltpu.make_async_copy(given[i], kept[i], sem.at[i]) for i in range(4)]
    writes = [pltpu.make_async_copy(kept[i], out[i], sem.at[4 + i]) for i in range(4)]
    for copy in reads:
        copy.start()
    for read, write in zip(reads, writes, strict=True):
        read.wait()
        write.start()
    for copy in writes:
        copy.wait()


def body(queries, keys, values, out_grad, out_weight, window, counts):
    hbm = pl.BlockSpec(memory_space=pl.ANY)
    vmem = pl.BlockSpec(memory_space=pltpu.VMEM)
    smem = pl.BlockSpec(memory_space=pltpu.SMEM)
    V = pltpu.VMEM
    dma = pltpu.SemaphoreType.DMA
    block = jax.ShapeDtypeStruct((TOK, COLS), BF16)
    scratch = [
        V((3, HEADS_HERE, TOK, HEAD_DIM), BF16),
        V((3, HEADS_HERE, TOK, HEAD_DIM), BF16),
        V((3, HEADS_HERE, TOK, HEAD_DIM), BF16),
        V((TOK, COLS), BF16),
        V((COLS, TP * COLS), BF16),
        V((TP, COLS, TOK), BF16),
        V((3, HEADS_HERE, HEAD_DIM, TOK), BF16),
        V((3, HEADS_HERE, HEAD_DIM, TOK), BF16),
        V((HEADS_HERE, 3, 2, SPAN, HALF), BF16),
        V((2, HEADS_HERE, 2, SPAN, HALF), BF16),
        V((3, SPAN, HALF), F32),
        V((2, 16, HALF), F32),
        V((2, 2, 8, HALF), F32),
        V((3, 8, TOK), F32),
        V((COLS, TOK), BF16),
        V((TOK, COLS), BF16),
        V((HEADS_HERE, 1, TOK), F32),
        V((3, 8, TOK), F32),
        V((COLS, TOK), F32),
        V((3, HEADS_HERE, HEAD_DIM, TOK), BF16),
        V((HEADS_HERE, TOK, HALF), F32),
        V((COLS, COLS), F32),
        V((16, STRIP, COLS), F32),
        V((16, STRIP, COLS), BF16),
        V((16, STRIP, COLS), BF16),
        V((2, 2, 4, STRIP, COLS), BF16),
        V((2, 2, 4, STRIP, COLS), BF16),
        V((2, 2, STRIP, COLS), BF16),
        V((STRIP, COLS), BF16),
        V((STRIP, COLS), BF16),
        dma((11,)),
        dma((12,)), dma((12,)),
        dma((GATHERS,)), dma((GATHERS,)),
        dma((6,)), dma((6,)),
        dma((4,)), dma((4,)),
        dma((6,)), dma((6,)),
        dma((8,)), dma((8,)),
        dma((16,)), dma((16,)),
        dma((4,)),
        dma((1,)), dma((1,)),
    ]
    dq, dk, dv, wg = pl.pallas_call(
        kernel,
        out_shape=(block, block, block, jax.ShapeDtypeStruct((STRIP, COLS), BF16)),
        in_specs=[smem, smem, hbm, hbm, hbm, hbm, hbm],
        out_specs=(vmem, vmem, vmem, vmem),
        scratch_shapes=scratch,
        compiler_params=pltpu.CompilerParams(
            collective_id=0, has_side_effects=True, vmem_limit_bytes=56 * 1024 * 1024
        ),
    )(window.T, counts, queries, keys, values, out_grad, out_weight)
    results = (dq, dk, dv, wg)
    dq, dk, dv, wg = pl.pallas_call(
        copy_out,
        out_shape=tuple(jax.ShapeDtypeStruct(r.shape, BF16) for r in results),
        in_specs=[hbm] * 4,
        out_specs=(hbm,) * 4,
        scratch_shapes=[V(r.shape, BF16) for r in results] + [dma((8,))],
    )(*results)
    return dq, dk, dv, wg.T


def solution(mesh):
    in_specs = (
        P("lon", "tp"),
        P("lon", "tp"),
        P("lon", "tp"),
        P("lon", "tp"),
        P("tp", None),
        P(),
        P(),
    )
    out_specs = (P("lon", "tp"), P("lon", "tp"), P("lon", "tp"), P("tp", "lon"))
    return jax.shard_map(body, mesh=mesh, in_specs=in_specs, out_specs=out_specs, check_vma=False)
```
